32 devices in a mesh: tok: 32 (over z, y, x, core), tp: 1.
Axes of the slice: x: 2, y: 2, z: 4, core: 2. Of those that a mesh axis runs over, the one named last changes fastest.
Arguments:
- tokens: bfloat16 [4096, 4096], P('tok', 'tp'), may hold values from -6 to 6
- w_query: bfloat16 [4096, 4096], P('tok', 'tp'), may hold values from -0.09375 to 0.09375
- w_key: bfloat16 [4096, 4096], P('tok', 'tp'), may hold values from -0.09375 to 0.09375
- w_value: bfloat16 [4096, 4096], P('tok', 'tp'), may hold values from -0.09375 to 0.09375
- short_taps: float32 [3, 3, 4096], P(None, None, 'tp'), may hold values from -3.5 to 3.5
- filters: float32 [4096, 4096], P(('tp', 'tok')), may hold values from -90 to 90, as said below
- skip_gain: float32 [4096], P(('tp', 'tok')), may hold values from 0.1 to 1.9
Outputs:
- layer_out: bfloat16 [4096, 4096], P('tok', 'tp')
The draws below stay inside these ranges and needn't reach their ends.
Inputs may be any that keep to these rules, and one draw needn't show every extreme that they name: `filters`: real-valued filter taps.
All inputs are finite; a program needn't handle non-finite values.
Results may differ from the reference program's by a relative error of at most 0.009.
Values may be sent and summed in bfloat16 or wider, within the bound.
A program may use at most 192 MiB of HBM per device.

```python
import math
import jax
import jax.numpy as jnp
from jax import lax

D = 4096
SEQ = 4096


def draw_filters(key, part):
    first, second, third, fourth = jax.random.split(key, 4)
    base = jnp.clip(jax.random.normal(first, (D, SEQ), jnp.float32), -6.0, 6.0)
    channel = jnp.exp(jax.random.uniform(second, (D, 1), jnp.float32, 0.0, math.log(10.0)))
    rough = jax.random.uniform(third, (1, SEQ), jnp.float32, 0.5, 1.5)
    rate = jax.random.uniform(fourth, (D, 1), jnp.float32, 0.0, 3.0)
    place = jnp.arange(SEQ, dtype=jnp.float32)[None, :] / SEQ
    return base * channel * rough * jnp.exp(-rate * place)


def block_scale(key, dims, shards, low, top_value):
    def one(dim, shards_of):
        draws = jax.random.uniform(jax.random.fold_in(jax.random.fold_in(key, 6), dim), (shards_of,), jnp.float32, low / len(shards), top_value / len(shards))
        return jnp.repeat(jnp.exp(draws), dims[dim] // shards_of).reshape((-1,) + (1,) * (len(dims) - dim - 1))

    loudness = one(*shards[0])
    for cut in shards[1:]:
        loudness = loudness * one(*cut)
    return loudness


def bell_draw(stream_key, dims, scale, reach, cuts=(), kind=jnp.bfloat16):
    factor_of = block_scale(stream_key, dims, cuts, -0.22, 0.18) if cuts else 1.0
    entries = jax.random.normal(stream_key, dims, jnp.float32) * scale * factor_of
    return jnp.minimum(jnp.maximum(entries, -reach), reach).astype(kind)


def setup_inputs(seed: int = 0) -> dict:
    seeds = jax.random.split(jax.random.key(seed), 8)
    tokens = bell_draw(seeds[0], (SEQ, D), 1.0, 6.0, ((0, 32),))
    w_query = bell_draw(seeds[1], (D, D), D ** -0.5, 0.09375, ((0, 32),))
    w_key = bell_draw(seeds[2], (D, D), D ** -0.5, 0.09375, ((0, 32),))
    w_value = bell_draw(seeds[3], (D, D), D ** -0.5, 0.09375, ((0, 32),))
    short_taps = bell_draw(seeds[4], (3, 3, D), 3 ** -0.5, 3.5, (), jnp.float32)
    filters = draw_filters(jax.random.fold_in(seeds[7], 71), 0)
    skip_gain = jnp.clip(1.0 + 0.18 * jax.random.normal(seeds[6], (D,), jnp.float32), 0.1, 1.9)
    return dict(tokens=tokens, w_query=w_query, w_key=w_key, w_value=w_value, short_taps=short_taps, filters=filters, skip_gain=skip_gain)


def short_conv(raw, taps):
    padded = jnp.pad(raw, ((2, 0), (0, 0)))
    return taps[0][None, :] * raw + taps[1][None, :] * padded[1:-1] + taps[2][None, :] * padded[:-2]

def reference(tokens, w_query, w_key, w_value, short_taps, filters, skip_gain):
    query_raw = jnp.dot(tokens, w_query, preferred_element_type=jnp.float32)
    query = short_conv(query_raw, short_taps[0]).astype(jnp.bfloat16)
    query = lax.optimization_barrier(query)
    keyed = short_conv(jnp.dot(tokens, w_key, preferred_element_type=jnp.float32), short_taps[1])
    valued = short_conv(jnp.dot(tokens, w_value, preferred_element_type=jnp.float32), short_taps[2])
    key_value = (keyed * valued).astype(jnp.bfloat16)
    key_value = lax.optimization_barrier(key_value)
    length = tokens.shape[0]
    signal = key_value.astype(jnp.float32).T
    width = signal.shape[0]
    block = math.gcd(width, 256)

    def convolve(pair):
        series, taps = pair
        unit = taps / jnp.sqrt(lax.optimization_barrier(jnp.sum(taps * taps, axis=1, keepdims=True)) + 1e-06)
        spectrum = jnp.fft.rfft(series, n=2 * length, axis=1) * jnp.fft.rfft(unit, n=2 * length, axis=1)
        return jnp.fft.irfft(spectrum, n=2 * length, axis=1)[:, :length]
    convolved = lax.map(convolve, (signal.reshape(width // block, block, length), filters.reshape(width // block, block, length)))
    convolved = convolved.reshape(width, length)
    mixed = (convolved + skip_gain[:, None] * signal).astype(jnp.bfloat16)
    mixed = lax.optimization_barrier(mixed)
    return (query.astype(jnp.float32) * mixed.T.astype(jnp.float32)).astype(jnp.bfloat16)
```

```python
import math

import jax
import jax.numpy as jnp
from jax import lax
from jax.sharding import PartitionSpec as P


def passed_along(value, axis, steps):
    count = lax.axis_size(axis)
    leading, last = (max(0, -steps), min(count, count - steps))
    return lax.ppermute(value, axis, [(source, source + steps) for source in range(leading, last)])


def split_lengths(length):
    inner = 1
    divisor = 1
    while divisor * divisor <= length:
        if length % divisor == 0:
            inner = divisor
        divisor += 1
    return (2 * length // inner, inner)


def angle_table(rows_count, cols_count, period):
    product = lax.broadcasted_iota(jnp.int32, (rows_count, cols_count), 0) * lax.broadcasted_iota(
        jnp.int32, (rows_count, cols_count), 1
    )
    theta = (product % period).astype(jnp.float32) * (2.0 * math.pi / period)
    return (jnp.cos(theta), jnp.sin(theta))


def forward_transform(signal, outer, inner):
    channels = signal.shape[0]
    precise = lax.Precision.HIGHEST
    cos_outer, sin_outer = angle_table(outer, outer, outer)
    blocks = signal.reshape(channels, outer // 2, inner)
    cos_outer = cos_outer[:, : outer // 2]
    sin_outer = sin_outer[:, : outer // 2]
    first_re = jnp.einsum("kn,cnb->ckb", cos_outer, blocks, precision=precise)
    first_im = -jnp.einsum("kn,cnb->ckb", sin_outer, blocks, precision=precise)
    cos_twist, sin_twist = angle_table(outer, inner, outer * inner)
    twist_re = first_re * cos_twist + first_im * sin_twist
    twist_im = first_im * cos_twist - first_re * sin_twist
    cos_inner, sin_inner = angle_table(inner, inner, inner)
    spec_re = jnp.einsum("ckn,nm->ckm", twist_re, cos_inner, precision=precise) + jnp.einsum(
        "ckn,nm->ckm", twist_im, sin_inner, precision=precise
    )
    spec_im = jnp.einsum("ckn,nm->ckm", twist_im, cos_inner, precision=precise) - jnp.einsum(
        "ckn,nm->ckm", twist_re, sin_inner, precision=precise
    )
    return (spec_re, spec_im)


def inverse_transform(spec_re, spec_im, outer, inner):
    channels = spec_re.shape[0]
    precise = lax.Precision.HIGHEST
    cos_inner, sin_inner = angle_table(inner, inner, inner)
    back_re = jnp.einsum("ckm,mn->ckn", spec_re, cos_inner, precision=precise) - jnp.einsum(
        "ckm,mn->ckn", spec_im, sin_inner, precision=precise
    )
    back_im = jnp.einsum("ckm,mn->ckn", spec_re, sin_inner, precision=precise) + jnp.einsum(
        "ckm,mn->ckn", spec_im, cos_inner, precision=precise
    )
    cos_twist, sin_twist = angle_table(outer, inner, outer * inner)
    turned_re = back_re * cos_twist - back_im * sin_twist
    turned_im = back_re * sin_twist + back_im * cos_twist
    cos_outer, sin_outer = angle_table(outer, outer, outer)
    cos_outer = cos_outer[: outer // 2]
    sin_outer = sin_outer[: outer // 2]
    result = jnp.einsum("nk,ckb->cnb", cos_outer, turned_re, precision=precise) - jnp.einsum(
        "nk,ckb->cnb", sin_outer, turned_im, precision=precise
    )
    result = result * (1.0 / (outer * inner))
    return result.reshape(channels, outer // 2 * inner)


def short_conv(cols, earlier, taps):
    extended = jnp.concatenate([earlier, cols], axis=1)
    return (
        taps[0][:, None] * extended[:, 2:]
        + taps[1][:, None] * extended[:, 1:-1]
        + taps[2][:, None] * extended[:, :-2]
    )


def local_by_tokens(tokens, w_query, w_key, w_value, short_taps, filters, skip_gain):
    gathered = lax.all_gather(tokens, "tp", axis=1, tiled=True)
    pieces = (
        lax.all_gather(w_query, "tok", axis=0, tiled=True),
        lax.all_gather(w_key, "tok", axis=0, tiled=True),
        lax.all_gather(w_value, "tok", axis=0, tiled=True),
    )
    query_cols, key_cols, value_cols = tuple(
        (
            lax.dot_general(
                piece, gathered, (((0,), (1,)), ((), ())), preferred_element_type=jnp.float32
            )
            for piece in pieces
        )
    )
    query_prev, key_prev, value_prev = passed_along(
        (query_cols[:, -2:], key_cols[:, -2:], value_cols[:, -2:]), "tok", 1
    )
    query = short_conv(query_cols, query_prev, short_taps[0]).astype(jnp.bfloat16)
    keyed = short_conv(key_cols, key_prev, short_taps[1])
    valued = short_conv(value_cols, value_prev, short_taps[2])
    key_value = (keyed * valued).astype(jnp.bfloat16)
    owned = lax.all_to_all(key_value, "tok", split_axis=0, concat_axis=1, tiled=True)
    signal = owned.astype(jnp.float32)
    length = signal.shape[1]
    outer, inner = split_lengths(length)
    unit = filters / jnp.sqrt(jnp.sum(filters * filters, axis=1, keepdims=True) + 1e-06)
    sig_re, sig_im = forward_transform(signal, outer, inner)
    filt_re, filt_im = forward_transform(unit, outer, inner)
    prod_re = sig_re * filt_re - sig_im * filt_im
    prod_im = sig_re * filt_im + sig_im * filt_re
    convolved = inverse_transform(prod_re, prod_im, outer, inner)
    mixed = (convolved + skip_gain[:, None] * signal).astype(jnp.bfloat16)
    returned = lax.all_to_all(mixed, "tok", split_axis=1, concat_axis=0, tiled=True)
    result = (query.astype(jnp.float32) * returned.astype(jnp.float32)).astype(jnp.bfloat16)
    return result.T


def unit_circle(phase, period):
    theta = (phase % period).astype(jnp.float32) * (2.0 * math.pi / period)
    return (jnp.cos(theta), jnp.sin(theta))


def quarter_tables(outer, inner):
    length = outer * inner
    iota = lax.broadcasted_iota
    k1 = iota(jnp.int32, (outer, outer), 0)
    n1 = iota(jnp.int32, (outer, outer), 1)
    cos1, sin1 = unit_circle((4 * k1 + 1) * n1, 4 * outer)
    outer_fwd = jnp.stack([cos1, -sin1], axis=1).reshape(2 * outer, outer)
    outer_inv = jnp.stack([cos1, -sin1], axis=1).reshape(2 * outer, outer).T
    k1 = iota(jnp.int32, (outer, inner), 0)
    n2 = iota(jnp.int32, (outer, inner), 1)
    twist = unit_circle((4 * k1 + 1) * n2, 4 * length)
    k2 = iota(jnp.int32, (inner, inner), 0)
    n2 = iota(jnp.int32, (inner, inner), 1)
    cos2, sin2 = unit_circle(k2 * n2, inner)
    inner_fwd = jnp.concatenate(
        [jnp.concatenate([cos2, sin2], 1), jnp.concatenate([-sin2, cos2], 1)], 0
    )
    inner_inv = jnp.concatenate(
        [jnp.concatenate([cos2, -sin2], 1), jnp.concatenate([sin2, cos2], 1)], 0
    )
    return outer_fwd, outer_inv, twist, inner_fwd, inner_inv * (1.0 / length)


def mul16(spec, a, b):
    return jnp.einsum(
        spec, a.astype(jnp.bfloat16), b.astype(jnp.bfloat16), preferred_element_type=jnp.float32
    )


def quarter_forward(signal, tables, outer, inner):
    outer_fwd, _, (cos_t, sin_t), inner_fwd, _ = tables
    channels = signal.shape[1]
    first = mul16("kn,nc->kc", outer_fwd, signal.reshape(outer, inner * channels))
    first = first.reshape(outer, 2, inner, channels)
    re, im = first[:, 0], first[:, 1]
    cos_t, sin_t = cos_t[:, :, None], sin_t[:, :, None]
    turned = jnp.concatenate([re * cos_t + im * sin_t, im * cos_t - re * sin_t], axis=1)
    return mul16("mn,knc->kmc", inner_fwd, turned).reshape(outer, 2, inner, channels)


def quarter_inverse(spec_re, spec_im, tables, outer, inner):
    _, outer_inv, (cos_t, sin_t), _, inner_inv = tables
    channels = spec_re.shape[2]
    spectrum = jnp.concatenate([spec_re, spec_im], axis=1)
    back = mul16("mn,knc->kmc", inner_inv, spectrum).reshape(outer, 2, inner, channels)
    re, im = back[:, 0], back[:, 1]
    cos_t, sin_t = cos_t[:, :, None], sin_t[:, :, None]
    turned = jnp.stack([re * cos_t - im * sin_t, re * sin_t + im * cos_t], axis=1)
    result = mul16("nk,kc->nc", outer_inv, turned.reshape(2 * outer, inner * channels))
    return result.reshape(outer * inner, channels)


def balanced(length):
    inner = max(d for d in range(1, int(math.isqrt(length)) + 1) if length % d == 0)
    return (length // inner, inner)


def long_conv(signal, filters_t, tables, outer, inner):
    unit = filters_t * lax.rsqrt(jnp.sum(filters_t * filters_t, axis=0, keepdims=True) + 1e-06)
    filt = quarter_forward(unit, tables, outer, inner)
    sig = quarter_forward(signal, tables, outer, inner)
    sig_re, sig_im, filt_re, filt_im = sig[:, 0], sig[:, 1], filt[:, 0], filt[:, 1]
    prod_re = sig_re * filt_re - sig_im * filt_im
    prod_im = sig_re * filt_im + sig_im * filt_re
    return quarter_inverse(prod_re, prod_im, tables, outer, inner)


def short_rows(raw, taps):
    padded = jnp.pad(raw, ((2, 0), (0, 0)))
    return taps[0] * raw + taps[1] * padded[1:-1] + taps[2] * padded[:-2]


def local_by_channels(tokens, w_query, w_key, w_value, short_taps, filters, skip_gain):
    owned = filters.shape[0]
    start = lax.axis_index("tok") * owned
    gathered = lax.all_gather(tokens, "tok", axis=0, tiled=True)
    weights = jnp.stack([w_query, w_key, w_value])
    weights = lax.all_to_all(weights, "tok", split_axis=2, concat_axis=1, tiled=True)
    raw = jnp.einsum("tk,pkc->ptc", gathered, weights, preferred_element_type=jnp.float32)
    taps = lax.dynamic_slice_in_dim(short_taps, start, owned, axis=2)
    query = short_rows(raw[0], taps[0]).astype(jnp.bfloat16)
    key_value = (short_rows(raw[1], taps[1]) * short_rows(raw[2], taps[2])).astype(jnp.bfloat16)
    outer, inner = balanced(filters.shape[1])
    tables = quarter_tables(outer, inner)
    convolved = long_conv(key_value, filters.T, tables, outer, inner)
    mixed = (convolved + skip_gain[None, :] * key_value.astype(jnp.float32)).astype(jnp.bfloat16)
    result = (query.astype(jnp.float32) * mixed.astype(jnp.float32)).astype(jnp.bfloat16)
    return lax.all_to_all(result, "tok", split_axis=0, concat_axis=1, tiled=True)


def solution(mesh):
    in_specs = (
        P("tok", "tp"),
        P("tok", "tp"),
        P("tok", "tp"),
        P("tok", "tp"),
        P(None, None, "tp"),
        P(("tp", "tok"), None),
        P(("tp", "tok")),
    )
    out_specs = P("tok", "tp")
    local = local_by_channels if mesh.shape["tp"] == 1 else local_by_tokens
    return jax.shard_map(local, mesh=mesh, in_specs=in_specs, out_specs=out_specs, check_vma=False)
```

```python
import functools
import math

import jax
import jax.numpy as jnp
from jax import lax
from jax.experimental import pallas as pl
from jax.experimental.pallas import tpu as pltpu
from jax.sharding import PartitionSpec as P


def passed_along(value, axis, steps):
    count = lax.axis_size(axis)
    leading, last = (max(0, -steps), min(count, count - steps))
    return lax.ppermute(value, axis, [(source, source + steps) for source in range(leading, last)])


def split_lengths(length):
    inner = 1
    divisor = 1
    while divisor * divisor <= length:
        if length % divisor == 0:
            inner = divisor
        divisor += 1
    return (2 * length // inner, inner)


def angle_table(rows_count, cols_count, period):
    product = lax.broadcasted_iota(jnp.int32, (rows_count, cols_count), 0) * lax.broadcasted_iota(
        jnp.int32, (rows_count, cols_count), 1
    )
    theta = (product % period).astype(jnp.float32) * (2.0 * math.pi / period)
    return (jnp.cos(theta), jnp.sin(theta))


def forward_transform(signal, outer, inner):
    channels = signal.shape[0]
    precise = lax.Precision.HIGHEST
    cos_outer, sin_outer = angle_table(outer, outer, outer)
    blocks = signal.reshape(channels, outer // 2, inner)
    cos_outer = cos_outer[:, : outer // 2]
    sin_outer = sin_outer[:, : outer // 2]
    first_re = jnp.einsum("kn,cnb->ckb", cos_outer, blocks, precision=precise)
    first_im = -jnp.einsum("kn,cnb->ckb", sin_outer, blocks, precision=precise)
    cos_twist, sin_twist = angle_table(outer, inner, outer * inner)
    twist_re = first_re * cos_twist + first_im * sin_twist
    twist_im = first_im * cos_twist - first_re * sin_twist
    cos_inner, sin_inner = angle_table(inner, inner, inner)
    spec_re = jnp.einsum("ckn,nm->ckm", twist_re, cos_inner, precision=precise) + jnp.einsum(
        "ckn,nm->ckm", twist_im, sin_inner, precision=precise
    )
    spec_im = jnp.einsum("ckn,nm->ckm", twist_im, cos_inner, precision=precise) - jnp.einsum(
        "ckn,nm->ckm", twist_re, sin_inner, precision=precise
    )
    return (spec_re, spec_im)


def inverse_transform(spec_re, spec_im, outer, inner):
    channels = spec_re.shape[0]
    precise = lax.Precision.HIGHEST
    cos_inner, sin_inner = angle_table(inner, inner, inner)
    back_re = jnp.einsum("ckm,mn->ckn", spec_re, cos_inner, precision=precise) - jnp.einsum(
        "ckm,mn->ckn", spec_im, sin_inner, precision=precise
    )
    back_im = jnp.einsum("ckm,mn->ckn", spec_re, sin_inner, precision=precise) + jnp.einsum(
        "ckm,mn->ckn", spec_im, cos_inner, precision=precise
    )
    cos_twist, sin_twist = angle_table(outer, inner, outer * inner)
    turned_re = back_re * cos_twist - back_im * sin_twist
    turned_im = back_re * sin_twist + back_im * cos_twist
    cos_outer, sin_outer = angle_table(outer, outer, outer)
    cos_outer = cos_outer[: outer // 2]
    sin_outer = sin_outer[: outer // 2]
    result = jnp.einsum("nk,ckb->cnb", cos_outer, turned_re, precision=precise) - jnp.einsum(
        "nk,ckb->cnb", sin_outer, turned_im, precision=precise
    )
    result = result * (1.0 / (outer * inner))
    return result.reshape(channels, outer // 2 * inner)


def short_conv(cols, earlier, taps):
    extended = jnp.concatenate([earlier, cols], axis=1)
    return (
        taps[0][:, None] * extended[:, 2:]
        + taps[1][:, None] * extended[:, 1:-1]
        + taps[2][:, None] * extended[:, :-2]
    )


def local_by_tokens(tokens, w_query, w_key, w_value, short_taps, filters, skip_gain):
    gathered = lax.all_gather(tokens, "tp", axis=1, tiled=True)
    pieces = (
        lax.all_gather(w_query, "tok", axis=0, tiled=True),
        lax.all_gather(w_key, "tok", axis=0, tiled=True),
        lax.all_gather(w_value, "tok", axis=0, tiled=True),
    )
    query_cols, key_cols, value_cols = tuple(
        (
            lax.dot_general(
                piece, gathered, (((0,), (1,)), ((), ())), preferred_element_type=jnp.float32
            )
            for piece in pieces
        )
    )
    query_prev, key_prev, value_prev = passed_along(
        (query_cols[:, -2:], key_cols[:, -2:], value_cols[:, -2:]), "tok", 1
    )
    query = short_conv(query_cols, query_prev, short_taps[0]).astype(jnp.bfloat16)
    keyed = short_conv(key_cols, key_prev, short_taps[1])
    valued = short_conv(value_cols, value_prev, short_taps[2])
    key_value = (keyed * valued).astype(jnp.bfloat16)
    owned = lax.all_to_all(key_value, "tok", split_axis=0, concat_axis=1, tiled=True)
    signal = owned.astype(jnp.float32)
    length = signal.shape[1]
    outer, inner = split_lengths(length)
    unit = filters / jnp.sqrt(jnp.sum(filters * filters, axis=1, keepdims=True) + 1e-06)
    sig_re, sig_im = forward_transform(signal, outer, inner)
    filt_re, filt_im = forward_transform(unit, outer, inner)
    prod_re = sig_re * filt_re - sig_im * filt_im
    prod_im = sig_re * filt_im + sig_im * filt_re
    convolved = inverse_transform(prod_re, prod_im, outer, inner)
    mixed = (convolved + skip_gain[:, None] * signal).astype(jnp.bfloat16)
    returned = lax.all_to_all(mixed, "tok", split_axis=1, concat_axis=0, tiled=True)
    result = (query.astype(jnp.float32) * returned.astype(jnp.float32)).astype(jnp.bfloat16)
    return result.T


def unit_circle(phase, period):
    theta = (phase % period).astype(jnp.float32) * (2.0 * math.pi / period)
    return (jnp.cos(theta), jnp.sin(theta))


def quarter_tables(outer, inner):
    length = outer * inner
    iota = lax.broadcasted_iota
    k1 = iota(jnp.int32, (outer, outer), 0)
    n1 = iota(jnp.int32, (outer, outer), 1)
    cos1, sin1 = unit_circle((4 * k1 + 1) * n1, 4 * outer)
    outer_fwd = jnp.stack([cos1, -sin1], axis=1).reshape(2 * outer, outer)
    outer_inv = jnp.stack([cos1, -sin1], axis=1).reshape(2 * outer, outer).T
    k1 = iota(jnp.int32, (outer, inner), 0)
    n2 = iota(jnp.int32, (outer, inner), 1)
    twist = unit_circle((4 * k1 + 1) * n2, 4 * length)
    k2 = iota(jnp.int32, (inner, inner), 0)
    n2 = iota(jnp.int32, (inner, inner), 1)
    cos2, sin2 = unit_circle(k2 * n2, inner)
    inner_fwd = jnp.concatenate(
        [jnp.concatenate([cos2, sin2], 1), jnp.concatenate([-sin2, cos2], 1)], 0
    )
    inner_inv = jnp.concatenate(
        [jnp.concatenate([cos2, -sin2], 1), jnp.concatenate([sin2, cos2], 1)], 0
    )
    return outer_fwd, outer_inv, twist, inner_fwd, inner_inv * (1.0 / length)


def mul16(spec, a, b):
    return jnp.einsum(
        spec, a.astype(jnp.bfloat16), b.astype(jnp.bfloat16), preferred_element_type=jnp.float32
    )


def quarter_forward(signal, tables, outer, inner):
    outer_fwd, _, (cos_t, sin_t), inner_fwd, _ = tables
    channels = signal.shape[1]
    first = mul16("kn,nc->kc", outer_fwd, signal.reshape(outer, inner * channels))
    first = first.reshape(outer, 2, inner, channels)
    re, im = first[:, 0], first[:, 1]
    cos_t, sin_t = cos_t[:, :, None], sin_t[:, :, None]
    turned = jnp.concatenate([re * cos_t + im * sin_t, im * cos_t - re * sin_t], axis=1)
    return mul16("mn,knc->kmc", inner_fwd, turned).reshape(outer, 2, inner, channels)


def quarter_inverse(spec_re, spec_im, tables, outer, inner):
    _, outer_inv, (cos_t, sin_t), _, inner_inv = tables
    channels = spec_re.shape[2]
    spectrum = jnp.concatenate([spec_re, spec_im], axis=1)
    back = mul16("mn,knc->kmc", inner_inv, spectrum).reshape(outer, 2, inner, channels)
    re, im = back[:, 0], back[:, 1]
    cos_t, sin_t = cos_t[:, :, None], sin_t[:, :, None]
    turned = jnp.stack([re * cos_t - im * sin_t, re * sin_t + im * cos_t], axis=1)
    result = mul16("nk,kc->nc", outer_inv, turned.reshape(2 * outer, inner * channels))
    return result.reshape(outer * inner, channels)


def balanced(length):
    inner = max(d for d in range(1, int(math.isqrt(length)) + 1) if length % d == 0)
    return (length // inner, inner)


def long_conv(signal, filters_t, tables, outer, inner):
    unit = filters_t * lax.rsqrt(jnp.sum(filters_t * filters_t, axis=0, keepdims=True) + 1e-06)
    filt = quarter_forward(unit, tables, outer, inner)
    sig = quarter_forward(signal, tables, outer, inner)
    sig_re, sig_im, filt_re, filt_im = sig[:, 0], sig[:, 1], filt[:, 0], filt[:, 1]
    prod_re = sig_re * filt_re - sig_im * filt_im
    prod_im = sig_re * filt_im + sig_im * filt_re
    return quarter_inverse(prod_re, prod_im, tables, outer, inner)


def exchange_kernel(
    count, tok_ref, w_ref, all_tok, all_w, send_sem, recv_sem, w_send, w_recv, local_sem
):
    me = lax.axis_index("tok")
    depth = count // 8
    core, x, y, z = (lax.rem(me, 2), lax.rem(me // 2, 2), lax.rem(me // 4, 2), me // 8)
    step_core, step_x, step_y = (1 - 2 * core, 2 - 4 * x, 4 - 8 * y)
    rows = tok_ref.shape[0] // 2

    barrier = pltpu.get_barrier_semaphore()

    @pl.loop(1, count)
    def _(j):
        pl.semaphore_signal(
            barrier,
            inc=1,
            device_id={"tok": lax.rem(me + j, count)},
            device_id_type=pl.DeviceIdType.MESH,
        )

    pl.semaphore_wait(barrier, count - 1)

    own_tok = pltpu.make_async_copy(tok_ref, all_tok.at[me], local_sem.at[0])
    own_w = pltpu.make_async_copy(w_ref.at[me], all_w.at[me], local_sem.at[1])
    own_tok.start()
    own_w.start()

    def tok_copy(half, block, dest, slot, own=False):
        part = pl.ds(half * rows, rows)
        return pltpu.make_async_remote_copy(
            src_ref=tok_ref.at[part] if own else all_tok.at[block, part],
            dst_ref=all_tok.at[block, part],
            send_sem=send_sem.at[half, block // 2, slot],
            recv_sem=recv_sem.at[half, block],
            device_id={"tok": dest},
            device_id_type=pl.DeviceIdType.MESH,
        )

    sent = []

    def put(cond, half, block, dest, slot, own=False):
        sent.append((cond, half, block, dest, slot))

        def go():
            tok_copy(half, block, dest, slot, own).start()

        go() if cond is None else pl.when(cond)(go)

    def arrived(cond, half, block):
        def go():
            tok_copy(half, block, me, 0).wait_recv()

        go() if cond is None else pl.when(cond)(go)

    turns = ((step_x, step_y), (step_y, step_x))
    for half in range(2):
        first, second = turns[half]
        put(z + 1 < depth, half, me, me + 8, 0, own=True)
        put(z > 0, half, me, me - 8, 1, own=True)
        put(None, half, me, me + first, 2, own=True)
        put(None, half, me, me + second, 3, own=True)
        put(None, half, me, me + step_core, 4, own=True)

    def w_copy(j):
        dest = lax.rem(me + j, count)
        return pltpu.make_async_remote_copy(
            src_ref=w_ref.at[dest],
            dst_ref=all_w.at[me],
            send_sem=w_send.at[j],
            recv_sem=w_recv.at[j],
            device_id={"tok": dest},
            device_id_type=pl.DeviceIdType.MESH,
        )

    pl.loop(1, count)(lambda j: w_copy(j).start())

    def both_ways(distance):
        yield (z >= distance, -8 * distance)
        if distance:
            yield (z + distance < depth, 8 * distance)

    def from_first(distance):
        for half in range(2):
            first, second = turns[half]
            for cond, shift in both_ways(distance):
                block = me + first + shift
                arrived(cond, half, block)
                put(cond, half, block, me + second, 3)
                put(cond, half, block, me + step_core, 4)

    for distance in range(1, depth):
        for half in range(2):
            first, second = turns[half]
            for cond, shift in both_ways(distance):
                block = me + shift
                arrived(cond, half, block)
                if shift < 0:
                    put(jnp.logical_and(cond, z + 1 < depth), half, block, me + 8, 0)
                else:
                    put(jnp.logical_and(cond, z > 0), half, block, me - 8, 1)
                put(cond, half, block, me + first, 2)
                put(cond, half, block, me + second, 3)
                put(cond, half, block, me + step_core, 4)
        from_first(distance - 1)
    from_first(depth - 1)
    for distance in range(depth):
        for half in range(2):
            first, second = turns[half]
            for cond, shift in both_ways(distance):
                for base in (second, first + second):
                    block = me + base + shift
                    arrived(cond, half, block)
                    put(cond, half, block, me + step_core, 4)

    @pl.loop(0, count // 2)
    def _(pair):
        for half in range(2):
            tok_copy(half, 2 * pair + 1 - core, me, 0).wait_recv()

    for cond, half, block, dest, slot in sent:

        def done(half=half, block=block, dest=dest, slot=slot):
            tok_copy(half, block, dest, slot).wait_send()

        done() if cond is None else pl.when(cond)(done)

    @pl.loop(1, count)
    def _(j):
        w_copy(j).wait_recv()
        w_copy(j).wait_send()

    own_tok.wait()
    own_w.wait()


def exchanged(tokens, weights):
    count = lax.axis_size("tok")
    anywhere = pl.BlockSpec(memory_space=pl.ANY)
    return pl.pallas_call(
        functools.partial(exchange_kernel, count),
        out_shape=(
            jax.ShapeDtypeStruct((count,) + tokens.shape, tokens.dtype),
            jax.ShapeDtypeStruct(weights.shape, weights.dtype),
        ),
        in_specs=[anywhere, anywhere],
        out_specs=(anywhere, anywhere),
        scratch_shapes=[
            pltpu.SemaphoreType.DMA((2, count // 2, 5)),
            pltpu.SemaphoreType.DMA((2, count)),
            pltpu.SemaphoreType.DMA((count,)),
            pltpu.SemaphoreType.DMA((count,)),
            pltpu.SemaphoreType.DMA((2,)),
        ],
        compiler_params=pltpu.CompilerParams(collective_id=0, has_side_effects=True),
    )(tokens, weights)


def gathered_and_columns(tokens, weights):
    count = lax.axis_size("tok")
    kinds, depth, channels = weights.shape
    blocks = weights.reshape(kinds, depth, count, channels // count)
    blocks = blocks.transpose(2, 1, 0, 3).reshape(count, depth, kinds * channels // count)
    if count % 8 == 0 and tokens.shape[0] % 32 == 0:
        all_tokens, columns = exchanged(tokens, blocks)
        all_tokens = all_tokens.reshape(count * tokens.shape[0], tokens.shape[1])
    else:
        all_tokens = lax.all_gather(tokens, "tok", axis=0, tiled=True)
        columns = lax.all_to_all(blocks, "tok", split_axis=0, concat_axis=0, tiled=True)
    return all_tokens, columns.reshape(count * depth, kinds * channels // count)


def short_rows(raw, taps):
    padded = jnp.pad(raw, ((2, 0), (0, 0)))
    return taps[0] * raw + taps[1] * padded[1:-1] + taps[2] * padded[:-2]


def local_by_channels(tokens, w_query, w_key, w_value, short_taps, filters, skip_gain):
    owned = filters.shape[0]
    start = lax.axis_index("tok") * owned
    gathered, columns = gathered_and_columns(tokens, jnp.stack([w_query, w_key, w_value]))
    raw = jnp.dot(gathered, columns, preferred_element_type=jnp.float32)
    raw = [raw[:, kind * owned : (kind + 1) * owned] for kind in range(3)]
    taps = lax.dynamic_slice_in_dim(short_taps, start, owned, axis=2)
    query = short_rows(raw[0], taps[0]).astype(jnp.bfloat16)
    key_value = (short_rows(raw[1], taps[1]) * short_rows(raw[2], taps[2])).astype(jnp.bfloat16)
    outer, inner = balanced(filters.shape[1])
    tables = quarter_tables(outer, inner)
    convolved = long_conv(key_value, filters.T, tables, outer, inner)
    mixed = (convolved + skip_gain[None, :] * key_value.astype(jnp.float32)).astype(jnp.bfloat16)
    result = (query.astype(jnp.float32) * mixed.astype(jnp.float32)).astype(jnp.bfloat16)
    return lax.all_to_all(result, "tok", split_axis=0, concat_axis=1, tiled=True)


def solution(mesh):
    in_specs = (
        P("tok", "tp"),
        P("tok", "tp"),
        P("tok", "tp"),
        P("tok", "tp"),
        P(None, None, "tp"),
        P(("tp", "tok"), None),
        P(("tp", "tok")),
    )
    out_specs = P("tok", "tp")
    local = local_by_channels if mesh.shape["tp"] == 1 else local_by_tokens
    return jax.shard_map(local, mesh=mesh, in_specs=in_specs, out_specs=out_specs, check_vma=False)
```

```python
import functools
import math

import jax
import jax.numpy as jnp
from jax import lax
from jax.experimental import pallas as pl
from jax.experimental.pallas import tpu as pltpu
from jax.sharding import PartitionSpec as P


def passed_along(value, axis, steps):
    count = lax.axis_size(axis)
    leading, last = (max(0, -steps), min(count, count - steps))
    return lax.ppermute(value, axis, [(source, source + steps) for source in range(leading, last)])


def split_lengths(length):
    inner = 1
    divisor = 1
    while divisor * divisor <= length:
        if length % divisor == 0:
            inner = divisor
        divisor += 1
    return (2 * length // inner, inner)


def angle_table(rows_count, cols_count, period):
    product = lax.broadcasted_iota(jnp.int32, (rows_count, cols_count), 0) * lax.broadcasted_iota(
        jnp.int32, (rows_count, cols_count), 1
    )
    theta = (product % period).astype(jnp.float32) * (2.0 * math.pi / period)
    return (jnp.cos(theta), jnp.sin(theta))


def forward_transform(signal, outer, inner):
    channels = signal.shape[0]
    precise = lax.Precision.HIGHEST
    cos_outer, sin_outer = angle_table(outer, outer, outer)
    blocks = signal.reshape(channels, outer // 2, inner)
    cos_outer = cos_outer[:, : outer // 2]
    sin_outer = sin_outer[:, : outer // 2]
    first_re = jnp.einsum("kn,cnb->ckb", cos_outer, blocks, precision=precise)
    first_im = -jnp.einsum("kn,cnb->ckb", sin_outer, blocks, precision=precise)
    cos_twist, sin_twist = angle_table(outer, inner, outer * inner)
    twist_re = first_re * cos_twist + first_im * sin_twist
    twist_im = first_im * cos_twist - first_re * sin_twist
    cos_inner, sin_inner = angle_table(inner, inner, inner)
    spec_re = jnp.einsum("ckn,nm->ckm", twist_re, cos_inner, precision=precise) + jnp.einsum(
        "ckn,nm->ckm", twist_im, sin_inner, precision=precise
    )
    spec_im = jnp.einsum("ckn,nm->ckm", twist_im, cos_inner, precision=precise) - jnp.einsum(
        "ckn,nm->ckm", twist_re, sin_inner, precision=precise
    )
    return (spec_re, spec_im)


def inverse_transform(spec_re, spec_im, outer, inner):
    channels = spec_re.shape[0]
    precise = lax.Precision.HIGHEST
    cos_inner, sin_inner = angle_table(inner, inner, inner)
    back_re = jnp.einsum("ckm,mn->ckn", spec_re, cos_inner, precision=precise) - jnp.einsum(
        "ckm,mn->ckn", spec_im, sin_inner, precision=precise
    )
    back_im = jnp.einsum("ckm,mn->ckn", spec_re, sin_inner, precision=precise) + jnp.einsum(
        "ckm,mn->ckn", spec_im, cos_inner, precision=precise
    )
    cos_twist, sin_twist = angle_table(outer, inner, outer * inner)
    turned_re = back_re * cos_twist - back_im * sin_twist
    turned_im = back_re * sin_twist + back_im * cos_twist
    cos_outer, sin_outer = angle_table(outer, outer, outer)
    cos_outer = cos_outer[: outer // 2]
    sin_outer = sin_outer[: outer // 2]
    result = jnp.einsum("nk,ckb->cnb", cos_outer, turned_re, precision=precise) - jnp.einsum(
        "nk,ckb->cnb", sin_outer, turned_im, precision=precise
    )
    result = result * (1.0 / (outer * inner))
    return result.reshape(channels, outer // 2 * inner)


def short_conv(cols, earlier, taps):
    extended = jnp.concatenate([earlier, cols], axis=1)
    return (
        taps[0][:, None] * extended[:, 2:]
        + taps[1][:, None] * extended[:, 1:-1]
        + taps[2][:, None] * extended[:, :-2]
    )


def local_by_tokens(tokens, w_query, w_key, w_value, short_taps, filters, skip_gain):
    gathered = lax.all_gather(tokens, "tp", axis=1, tiled=True)
    pieces = (
        lax.all_gather(w_query, "tok", axis=0, tiled=True),
        lax.all_gather(w_key, "tok", axis=0, tiled=True),
        lax.all_gather(w_value, "tok", axis=0, tiled=True),
    )
    query_cols, key_cols, value_cols = tuple(
        (
            lax.dot_general(
                piece, gathered, (((0,), (1,)), ((), ())), preferred_element_type=jnp.float32
            )
            for piece in pieces
        )
    )
    query_prev, key_prev, value_prev = passed_along(
        (query_cols[:, -2:], key_cols[:, -2:], value_cols[:, -2:]), "tok", 1
    )
    query = short_conv(query_cols, query_prev, short_taps[0]).astype(jnp.bfloat16)
    keyed = short_conv(key_cols, key_prev, short_taps[1])
    valued = short_conv(value_cols, value_prev, short_taps[2])
    key_value = (keyed * valued).astype(jnp.bfloat16)
    owned = lax.all_to_all(key_value, "tok", split_axis=0, concat_axis=1, tiled=True)
    signal = owned.astype(jnp.float32)
    length = signal.shape[1]
    outer, inner = split_lengths(length)
    unit = filters / jnp.sqrt(jnp.sum(filters * filters, axis=1, keepdims=True) + 1e-06)
    sig_re, sig_im = forward_transform(signal, outer, inner)
    filt_re, filt_im = forward_transform(unit, outer, inner)
    prod_re = sig_re * filt_re - sig_im * filt_im
    prod_im = sig_re * filt_im + sig_im * filt_re
    convolved = inverse_transform(prod_re, prod_im, outer, inner)
    mixed = (convolved + skip_gain[:, None] * signal).astype(jnp.bfloat16)
    returned = lax.all_to_all(mixed, "tok", split_axis=1, concat_axis=0, tiled=True)
    result = (query.astype(jnp.float32) * returned.astype(jnp.float32)).astype(jnp.bfloat16)
    return result.T


def unit_circle(phase, period):
    theta = (phase % period).astype(jnp.float32) * (2.0 * math.pi / period)
    return (jnp.cos(theta), jnp.sin(theta))


def quarter_tables(outer, inner):
    length = outer * inner
    iota = lax.broadcasted_iota
    k1 = iota(jnp.int32, (outer, outer), 0)
    n1 = iota(jnp.int32, (outer, outer), 1)
    cos1, sin1 = unit_circle((4 * k1 + 1) * n1, 4 * outer)
    outer_fwd = jnp.stack([cos1, -sin1], axis=1).reshape(2 * outer, outer)
    outer_inv = jnp.stack([cos1, -sin1], axis=1).reshape(2 * outer, outer).T
    k1 = iota(jnp.int32, (outer, inner), 0)
    n2 = iota(jnp.int32, (outer, inner), 1)
    twist = unit_circle((4 * k1 + 1) * n2, 4 * length)
    k2 = iota(jnp.int32, (inner, inner), 0)
    n2 = iota(jnp.int32, (inner, inner), 1)
    cos2, sin2 = unit_circle(k2 * n2, inner)
    inner_fwd = jnp.concatenate(
        [jnp.concatenate([cos2, sin2], 1), jnp.concatenate([-sin2, cos2], 1)], 0
    )
    inner_inv = jnp.concatenate(
        [jnp.concatenate([cos2, -sin2], 1), jnp.concatenate([sin2, cos2], 1)], 0
    )
    return outer_fwd, outer_inv, twist, inner_fwd, inner_inv * (1.0 / length)


def mul16(spec, a, b):
    return jnp.einsum(
        spec, a.astype(jnp.bfloat16), b.astype(jnp.bfloat16), preferred_element_type=jnp.float32
    )


def quarter_forward(signal, tables, outer, inner):
    outer_fwd, _, (cos_t, sin_t), inner_fwd, _ = tables
    channels = signal.shape[1]
    first = mul16("kn,nc->kc", outer_fwd, signal.reshape(outer, inner * channels))
    first = first.reshape(outer, 2, inner, channels)
    re, im = first[:, 0], first[:, 1]
    cos_t, sin_t = cos_t[:, :, None], sin_t[:, :, None]
    turned = jnp.concatenate([re * cos_t + im * sin_t, im * cos_t - re * sin_t], axis=1)
    return mul16("mn,knc->kmc", inner_fwd, turned).reshape(outer, 2, inner, channels)


def quarter_inverse(spec_re, spec_im, tables, outer, inner):
    _, outer_inv, (cos_t, sin_t), _, inner_inv = tables
    channels = spec_re.shape[2]
    spectrum = jnp.concatenate([spec_re, spec_im], axis=1)
    back = mul16("mn,knc->kmc", inner_inv, spectrum).reshape(outer, 2, inner, channels)
    re, im = back[:, 0], back[:, 1]
    cos_t, sin_t = cos_t[:, :, None], sin_t[:, :, None]
    turned = jnp.stack([re * cos_t - im * sin_t, re * sin_t + im * cos_t], axis=1)
    result = mul16("nk,kc->nc", outer_inv, turned.reshape(2 * outer, inner * channels))
    return result.reshape(outer * inner, channels)


def balanced(length):
    inner = max(d for d in range(1, int(math.isqrt(length)) + 1) if length % d == 0)
    return (length // inner, inner)


def long_conv(signal, filters_t, tables, outer, inner):
    unit = filters_t * lax.rsqrt(jnp.sum(filters_t * filters_t, axis=0, keepdims=True) + 1e-06)
    filt = quarter_forward(unit, tables, outer, inner)
    sig = quarter_forward(signal, tables, outer, inner)
    sig_re, sig_im, filt_re, filt_im = sig[:, 0], sig[:, 1], filt[:, 0], filt[:, 1]
    prod_re = sig_re * filt_re - sig_im * filt_im
    prod_im = sig_re * filt_im + sig_im * filt_re
    return quarter_inverse(prod_re, prod_im, tables, outer, inner)


def exchange_kernel(
    count,
    tok_ref,
    w_query,
    w_key,
    w_value,
    raw_ref,
    all_tok,
    columns,
    held,
    send_sem,
    recv_sem,
    w_send,
    w_recv,
    local_sem,
    held_sem,
):
    me = lax.axis_index("tok")
    depth = count // 8
    core, x, y, z = (lax.rem(me, 2), lax.rem(me // 2, 2), lax.rem(me // 4, 2), me // 8)
    step_core, step_x, step_y = (1 - 2 * core, 2 - 4 * x, 4 - 8 * y)
    rows = tok_ref.shape[0] // 2

    barrier = pltpu.get_barrier_semaphore()

    @pl.loop(1, count)
    def _(j):
        pl.semaphore_signal(
            barrier,
            inc=1,
            device_id={"tok": lax.rem(me + j, count)},
            device_id_type=pl.DeviceIdType.MESH,
        )

    pl.semaphore_wait(barrier, count - 1)

    own_tok = pltpu.make_async_copy(tok_ref, all_tok.at[me], local_sem.at[0])
    own_tok.start()
    weights = (w_query, w_key, w_value)
    w_rows = w_query.shape[0]
    w_cols = w_query.shape[1] // count

    def w_ends(kind, dest):
        src = weights[kind].at[:, pl.ds(pl.multiple_of(dest * w_cols, w_cols), w_cols)]
        landing = pl.ds(pl.multiple_of(me * w_rows, w_rows), w_rows)
        return src, columns.at[landing, pl.ds(kind * w_cols, w_cols)]

    own_w = [
        pltpu.make_async_copy(*w_ends(kind, me), local_sem.at[1 + kind]) for kind in range(3)
    ]
    for copy in own_w:
        copy.start()

    def tok_copy(half, block, dest, slot, own=False):
        part = pl.ds(half * rows, rows)
        return pltpu.make_async_remote_copy(
            src_ref=tok_ref.at[part] if own else all_tok.at[block, part],
            dst_ref=all_tok.at[block, part],
            send_sem=send_sem.at[half, block // 2, slot],
            recv_sem=recv_sem.at[half, block],
            device_id={"tok": dest},
            device_id_type=pl.DeviceIdType.MESH,
        )

    sent = []

    def put(cond, half, block, dest, slot, own=False):
        sent.append((cond, half, block, dest, slot))

        def go():
            tok_copy(half, block, dest, slot, own).start()

        go() if cond is None else pl.when(cond)(go)

    def arrived(cond, half, block):
        def go():
            tok_copy(half, block, me, 0).wait_recv()

        go() if cond is None else pl.when(cond)(go)

    turns = ((step_x, step_y), (step_y, step_x))
    for half in range(2):
        first, second = turns[half]
        put(z + 1 < depth, half, me, me + 8, 0, own=True)
        put(z > 0, half, me, me - 8, 1, own=True)
        put(None, half, me, me + first, 2, own=True)
        put(None, half, me, me + second, 3, own=True)
        put(None, half, me, me + step_core, 4, own=True)

    def w_copy(j, kind):
        dest = lax.rem(me + j, count)
        src, dst = w_ends(kind, dest)
        return pltpu.make_async_remote_copy(
            src_ref=src,
            dst_ref=dst,
            send_sem=w_send.at[kind, j],
            recv_sem=w_recv.at[kind, j],
            device_id={"tok": dest},
            device_id_type=pl.DeviceIdType.MESH,
        )

    @pl.loop(1, count)
    def _(j):
        for kind in range(3):
            w_copy(j, kind).start()

    def both_ways(distance):
        yield (z >= distance, -8 * distance)
        if distance:
            yield (z + distance < depth, 8 * distance)

    def from_first(distance):
        for half in range(2):
            first, second = turns[half]
            for cond, shift in both_ways(distance):
                block = me + first + shift
                arrived(cond, half, block)
                put(cond, half, block, me + second, 3)
                put(cond, half, block, me + step_core, 4)

    for distance in range(1, depth):
        for half in range(2):
            first, second = turns[half]
            for cond, shift in both_ways(distance):
                block = me + shift
                arrived(cond, half, block)
                if shift < 0:
                    put(jnp.logical_and(cond, z + 1 < depth), half, block, me + 8, 0)
                else:
                    put(jnp.logical_and(cond, z > 0), half, block, me - 8, 1)
                put(cond, half, block, me + first, 2)
                put(cond, half, block, me + second, 3)
                put(cond, half, block, me + step_core, 4)
        from_first(distance - 1)
    from_first(depth - 1)
    own_tok.wait()
    for copy in own_w:
        copy.wait()

    @pl.loop(1, count)
    def _(j):
        for kind in range(3):
            w_copy(j, kind).wait_recv()

    def last_leg(turn):
        distance = (turn + 1) // 2
        there = z + distance * (1 - 2 * lax.rem(turn, 2))
        return there, jnp.logical_and(there >= 0, there < depth)

    def to_core(half, there, base):
        block = there * 8 + lax.rem(me, 8) + base
        return tok_copy(half, block, me + step_core, 4)

    def load(there, k):
        block = there * 8 + 2 * lax.rem(k, 4) + jnp.where(k < 4, core, 1 - core)
        return block, pltpu.make_async_copy(all_tok.at[block], held.at[k], held_sem.at[k])

    block_rows = tok_ref.shape[0]

    @pl.loop(0, 2 * depth - 1)
    def _(turn):
        there, valid = last_leg(turn)

        @pl.when(valid)
        def _():
            for half in range(2):
                first, second = turns[half]
                for base in (second, first + second):
                    to_core(half, there, base).wait_recv()
                    to_core(half, there, base).start()

            @pl.loop(0, 4)
            def _(k):
                load(there, k)[1].start()

            @pl.loop(0, 8)
            def _(k):
                block, copy = load(there, k)

                @pl.when(k == 1)
                def _():
                    @pl.loop(0, 4)
                    def _(other):
                        later, later_copy = load(there, other + 4)
                        for half in range(2):
                            tok_copy(half, later, me, 0).wait_recv()
                        later_copy.start()

                copy.wait()
                place = pl.ds(pl.multiple_of(block * block_rows, block_rows), block_rows)
                raw_ref[place, :] = jnp.dot(
                    held[k], columns[...], preferred_element_type=jnp.float32
                )

    @pl.loop(0, 2 * depth - 1)
    def _(turn):
        there, valid = last_leg(turn)

        @pl.when(valid)
        def _():
            for half in range(2):
                first, second = turns[half]
                for base in (second, first + second):
                    to_core(half, there, base).wait_send()

    for cond, half, block, dest, slot in sent:

        def done(half=half, block=block, dest=dest, slot=slot):
            tok_copy(half, block, dest, slot).wait_send()

        done() if cond is None else pl.when(cond)(done)

    @pl.loop(1, count)
    def _(j):
        for kind in range(3):
            w_copy(j, kind).wait_send()


def exchanged(tokens, weights):
    count = lax.axis_size("tok")
    rows, width = tokens.shape
    w_rows, channels = weights[0].shape
    cols = 3 * channels // count
    anywhere = pl.BlockSpec(memory_space=pl.ANY)
    raw, _ = pl.pallas_call(
        functools.partial(exchange_kernel, count),
        out_shape=(
            jax.ShapeDtypeStruct((count * rows, cols), jnp.float32),
            jax.ShapeDtypeStruct((count, rows, width), tokens.dtype),
        ),
        in_specs=[anywhere] * 4,
        out_specs=(pl.BlockSpec(memory_space=pltpu.VMEM), anywhere),
        scratch_shapes=[
            pltpu.VMEM((count * w_rows, cols), weights[0].dtype),
            pltpu.VMEM((8, rows, width), tokens.dtype),
            pltpu.SemaphoreType.DMA((2, count // 2, 5)),
            pltpu.SemaphoreType.DMA((2, count)),
            pltpu.SemaphoreType.DMA((3, count)),
            pltpu.SemaphoreType.DMA((3, count)),
            pltpu.SemaphoreType.DMA((4,)),
            pltpu.SemaphoreType.DMA((8,)),
        ],
        compiler_params=pltpu.CompilerParams(
            collective_id=0, has_side_effects=True, vmem_limit_bytes=40 * 2**20
        ),
    )(tokens, *weights)
    return raw


def projected(tokens, weights):
    count = lax.axis_size("tok")
    rows = tokens.shape[0]
    w_rows, channels = weights[0].shape
    if count % 8 == 0 and rows % 32 == 0 and w_rows % 16 == 0 and channels % (128 * count) == 0:
        return exchanged(tokens, weights)
    gathered = lax.all_gather(tokens, "tok", axis=0, tiled=True)
    columns = [
        lax.all_to_all(weight, "tok", split_axis=1, concat_axis=0, tiled=True)
        for weight in weights
    ]
    return jnp.dot(
        gathered, jnp.concatenate(columns, axis=1), preferred_element_type=jnp.float32
    )


def short_rows(raw, taps):
    padded = jnp.pad(raw, ((2, 0), (0, 0)))
    return taps[0] * raw + taps[1] * padded[1:-1] + taps[2] * padded[:-2]


def local_by_channels(tokens, w_query, w_key, w_value, short_taps, filters, skip_gain):
    owned = filters.shape[0]
    start = lax.axis_index("tok") * owned
    raw = projected(tokens, (w_query, w_key, w_value))
    raw = [raw[:, kind * owned : (kind + 1) * owned] for kind in range(3)]
    taps = lax.dynamic_slice_in_dim(short_taps, start, owned, axis=2)
    query = short_rows(raw[0], taps[0]).astype(jnp.bfloat16)
    key_value = (short_rows(raw[1], taps[1]) * short_rows(raw[2], taps[2])).astype(jnp.bfloat16)
    outer, inner = balanced(filters.shape[1])
    tables = quarter_tables(outer, inner)
    convolved = long_conv(key_value, filters.T, tables, outer, inner)
    mixed = (convolved + skip_gain[None, :] * key_value.astype(jnp.float32)).astype(jnp.bfloat16)
    result = (query.astype(jnp.float32) * mixed.astype(jnp.float32)).astype(jnp.bfloat16)
    return lax.all_to_all(result, "tok", split_axis=0, concat_axis=1, tiled=True)


def solution(mesh):
    in_specs = (
        P("tok", "tp"),
        P("tok", "tp"),
        P("tok", "tp"),
        P("tok", "tp"),
        P(None, None, "tp"),
        P(("tp", "tok"), None),
        P(("tp", "tok")),
    )
    out_specs = P("tok", "tp")
    local = local_by_channels if mesh.shape["tp"] == 1 else local_by_tokens
    return jax.shard_map(local, mesh=mesh, in_specs=in_specs, out_specs=out_specs, check_vma=False)
```

```python
import functools
import math

import jax
import jax.numpy as jnp
from jax import lax
from jax.experimental import pallas as pl
from jax.experimental.pallas import tpu as pltpu
from jax.sharding import PartitionSpec as P


def passed_along(value, axis, steps):
    count = lax.axis_size(axis)
    leading, last = (max(0, -steps), min(count, count - steps))
    return lax.ppermute(value, axis, [(source, source + steps) for source in range(leading, last)])


def split_lengths(length):
    inner = 1
    divisor = 1
    while divisor * divisor <= length:
        if length % divisor == 0:
            inner = divisor
        divisor += 1
    return (2 * length // inner, inner)


def angle_table(rows_count, cols_count, period):
    product = lax.broadcasted_iota(jnp.int32, (rows_count, cols_count), 0) * lax.broadcasted_iota(
        jnp.int32, (rows_count, cols_count), 1
    )
    theta = (product % period).astype(jnp.float32) * (2.0 * math.pi / period)
    return (jnp.cos(theta), jnp.sin(theta))


def forward_transform(signal, outer, inner):
    channels = signal.shape[0]
    precise = lax.Precision.HIGHEST
    cos_outer, sin_outer = angle_table(outer, outer, outer)
    blocks = signal.reshape(channels, outer // 2, inner)
    cos_outer = cos_outer[:, : outer // 2]
    sin_outer = sin_outer[:, : outer // 2]
    first_re = jnp.einsum("kn,cnb->ckb", cos_outer, blocks, precision=precise)
    first_im = -jnp.einsum("kn,cnb->ckb", sin_outer, blocks, precision=precise)
    cos_twist, sin_twist = angle_table(outer, inner, outer * inner)
    twist_re = first_re * cos_twist + first_im * sin_twist
    twist_im = first_im * cos_twist - first_re * sin_twist
    cos_inner, sin_inner = angle_table(inner, inner, inner)
    spec_re = jnp.einsum("ckn,nm->ckm", twist_re, cos_inner, precision=precise) + jnp.einsum(
        "ckn,nm->ckm", twist_im, sin_inner, precision=precise
    )
    spec_im = jnp.einsum("ckn,nm->ckm", twist_im, cos_inner, precision=precise) - jnp.einsum(
        "ckn,nm->ckm", twist_re, sin_inner, precision=precise
    )
    return (spec_re, spec_im)


def inverse_transform(spec_re, spec_im, outer, inner):
    channels = spec_re.shape[0]
    precise = lax.Precision.HIGHEST
    cos_inner, sin_inner = angle_table(inner, inner, inner)
    back_re = jnp.einsum("ckm,mn->ckn", spec_re, cos_inner, precision=precise) - jnp.einsum(
        "ckm,mn->ckn", spec_im, sin_inner, precision=precise
    )
    back_im = jnp.einsum("ckm,mn->ckn", spec_re, sin_inner, precision=precise) + jnp.einsum(
        "ckm,mn->ckn", spec_im, cos_inner, precision=precise
    )
    cos_twist, sin_twist = angle_table(outer, inner, outer * inner)
    turned_re = back_re * cos_twist - back_im * sin_twist
    turned_im = back_re * sin_twist + back_im * cos_twist
    cos_outer, sin_outer = angle_table(outer, outer, outer)
    cos_outer = cos_outer[: outer // 2]
    sin_outer = sin_outer[: outer // 2]
    result = jnp.einsum("nk,ckb->cnb", cos_outer, turned_re, precision=precise) - jnp.einsum(
        "nk,ckb->cnb", sin_outer, turned_im, precision=precise
    )
    result = result * (1.0 / (outer * inner))
    return result.reshape(channels, outer // 2 * inner)


def short_conv(cols, earlier, taps):
    extended = jnp.concatenate([earlier, cols], axis=1)
    return (
        taps[0][:, None] * extended[:, 2:]
        + taps[1][:, None] * extended[:, 1:-1]
        + taps[2][:, None] * extended[:, :-2]
    )


def local_by_tokens(tokens, w_query, w_key, w_value, short_taps, filters, skip_gain):
    gathered = lax.all_gather(tokens, "tp", axis=1, tiled=True)
    pieces = (
        lax.all_gather(w_query, "tok", axis=0, tiled=True),
        lax.all_gather(w_key, "tok", axis=0, tiled=True),
        lax.all_gather(w_value, "tok", axis=0, tiled=True),
    )
    query_cols, key_cols, value_cols = tuple(
        (
            lax.dot_general(
                piece, gathered, (((0,), (1,)), ((), ())), preferred_element_type=jnp.float32
            )
            for piece in pieces
        )
    )
    query_prev, key_prev, value_prev = passed_along(
        (query_cols[:, -2:], key_cols[:, -2:], value_cols[:, -2:]), "tok", 1
    )
    query = short_conv(query_cols, query_prev, short_taps[0]).astype(jnp.bfloat16)
    keyed = short_conv(key_cols, key_prev, short_taps[1])
    valued = short_conv(value_cols, value_prev, short_taps[2])
    key_value = (keyed * valued).astype(jnp.bfloat16)
    owned = lax.all_to_all(key_value, "tok", split_axis=0, concat_axis=1, tiled=True)
    signal = owned.astype(jnp.float32)
    length = signal.shape[1]
    outer, inner = split_lengths(length)
    unit = filters / jnp.sqrt(jnp.sum(filters * filters, axis=1, keepdims=True) + 1e-06)
    sig_re, sig_im = forward_transform(signal, outer, inner)
    filt_re, filt_im = forward_transform(unit, outer, inner)
    prod_re = sig_re * filt_re - sig_im * filt_im
    prod_im = sig_re * filt_im + sig_im * filt_re
    convolved = inverse_transform(prod_re, prod_im, outer, inner)
    mixed = (convolved + skip_gain[:, None] * signal).astype(jnp.bfloat16)
    returned = lax.all_to_all(mixed, "tok", split_axis=1, concat_axis=0, tiled=True)
    result = (query.astype(jnp.float32) * returned.astype(jnp.float32)).astype(jnp.bfloat16)
    return result.T


def unit_circle(phase, period):
    theta = (phase % period).astype(jnp.float32) * (2.0 * math.pi / period)
    return (jnp.cos(theta), jnp.sin(theta))


def quarter_tables(outer, inner):
    length = outer * inner
    iota = lax.broadcasted_iota
    k1 = iota(jnp.int32, (outer, outer), 0)
    n1 = iota(jnp.int32, (outer, outer), 1)
    cos1, sin1 = unit_circle((4 * k1 + 1) * n1, 4 * outer)
    outer_fwd = jnp.stack([cos1, -sin1], axis=1).reshape(2 * outer, outer)
    outer_inv = jnp.stack([cos1, -sin1], axis=1).reshape(2 * outer, outer).T
    k1 = iota(jnp.int32, (outer, inner), 0)
    n2 = iota(jnp.int32, (outer, inner), 1)
    twist = unit_circle((4 * k1 + 1) * n2, 4 * length)
    k2 = iota(jnp.int32, (inner, inner), 0)
    n2 = iota(jnp.int32, (inner, inner), 1)
    cos2, sin2 = unit_circle(k2 * n2, inner)
    inner_fwd = jnp.concatenate(
        [jnp.concatenate([cos2, sin2], 1), jnp.concatenate([-sin2, cos2], 1)], 0
    )
    inner_inv = jnp.concatenate(
        [jnp.concatenate([cos2, -sin2], 1), jnp.concatenate([sin2, cos2], 1)], 0
    )
    return outer_fwd, outer_inv, twist, inner_fwd, inner_inv * (1.0 / length)


def mul16(spec, a, b):
    return jnp.einsum(
        spec, a.astype(jnp.bfloat16), b.astype(jnp.bfloat16), preferred_element_type=jnp.float32
    )


def quarter_forward(signal, tables, outer, inner):
    outer_fwd, _, (cos_t, sin_t), inner_fwd, _ = tables
    channels = signal.shape[1]
    first = mul16("kn,nc->kc", outer_fwd, signal.reshape(outer, inner * channels))
    first = first.reshape(outer, 2, inner, channels)
    re, im = first[:, 0], first[:, 1]
    cos_t, sin_t = cos_t[:, :, None], sin_t[:, :, None]
    turned = jnp.concatenate([re * cos_t + im * sin_t, im * cos_t - re * sin_t], axis=1)
    return mul16("mn,knc->kmc", inner_fwd, turned).reshape(outer, 2, inner, channels)


def quarter_inverse(spec_re, spec_im, tables, outer, inner):
    _, outer_inv, (cos_t, sin_t), _, inner_inv = tables
    channels = spec_re.shape[2]
    spectrum = jnp.concatenate([spec_re, spec_im], axis=1)
    back = mul16("mn,knc->kmc", inner_inv, spectrum).reshape(outer, 2, inner, channels)
    re, im = back[:, 0], back[:, 1]
    cos_t, sin_t = cos_t[:, :, None], sin_t[:, :, None]
    turned = jnp.stack([re * cos_t - im * sin_t, re * sin_t + im * cos_t], axis=1)
    result = mul16("nk,kc->nc", outer_inv, turned.reshape(2 * outer, inner * channels))
    return result.reshape(outer * inner, channels)


def balanced(length):
    inner = max(d for d in range(1, int(math.isqrt(length)) + 1) if length % d == 0)
    return (length // inner, inner)


def long_conv(signal, filters_t, tables, outer, inner):
    unit = filters_t * lax.rsqrt(jnp.sum(filters_t * filters_t, axis=0, keepdims=True) + 1e-06)
    filt = quarter_forward(unit, tables, outer, inner)
    sig = quarter_forward(signal, tables, outer, inner)
    sig_re, sig_im, filt_re, filt_im = sig[:, 0], sig[:, 1], filt[:, 0], filt[:, 1]
    prod_re = sig_re * filt_re - sig_im * filt_im
    prod_im = sig_re * filt_im + sig_im * filt_re
    return quarter_inverse(prod_re, prod_im, tables, outer, inner)


def exchange_kernel(
    count,
    tok_ref,
    w_query,
    w_key,
    w_value,
    raw_ref,
    all_tok,
    columns,
    held,
    send_sem,
    recv_sem,
    w_send,
    w_recv,
    local_sem,
    held_sem,
):
    me = lax.axis_index("tok")
    depth = count // 8
    core, x, y, z = (lax.rem(me, 2), lax.rem(me // 2, 2), lax.rem(me // 4, 2), me // 8)
    step_core, step_x, step_y = (1 - 2 * core, 2 - 4 * x, 4 - 8 * y)
    rows = tok_ref.shape[0] // 2

    barrier = pltpu.get_barrier_semaphore()

    @pl.loop(1, count)
    def _(j):
        pl.semaphore_signal(
            barrier,
            inc=1,
            device_id={"tok": lax.rem(me + j, count)},
            device_id_type=pl.DeviceIdType.MESH,
        )

    pl.semaphore_wait(barrier, count - 1)

    own_tok = pltpu.make_async_copy(tok_ref, all_tok.at[me], local_sem.at[0])
    own_tok.start()
    weights = (w_query, w_key, w_value)
    w_rows = w_query.shape[0]
    w_cols = w_query.shape[1] // count

    def w_ends(kind, dest):
        src = weights[kind].at[:, pl.ds(pl.multiple_of(dest * w_cols, w_cols), w_cols)]
        landing = pl.ds(pl.multiple_of(me * w_rows, w_rows), w_rows)
        return src, columns.at[landing, pl.ds(kind * w_cols, w_cols)]

    own_w = [
        pltpu.make_async_copy(*w_ends(kind, me), local_sem.at[1 + kind]) for kind in range(3)
    ]
    for copy in own_w:
        copy.start()

    def tok_copy(half, block, dest, slot, own=False):
        part = pl.ds(half * rows, rows)
        return pltpu.make_async_remote_copy(
            src_ref=tok_ref.at[part] if own else all_tok.at[block, part],
            dst_ref=all_tok.at[block, part],
            send_sem=send_sem.at[half, block // 2, slot],
            recv_sem=recv_sem.at[half, block],
            device_id={"tok": dest},
            device_id_type=pl.DeviceIdType.MESH,
        )

    sent = []

    def put(cond, half, block, dest, slot, own=False):
        sent.append((cond, half, block, dest, slot))

        def go():
            tok_copy(half, block, dest, slot, own).start()

        go() if cond is None else pl.when(cond)(go)

    def arrived(cond, half, block):
        def go():
            tok_copy(half, block, me, 0).wait_recv()

        go() if cond is None else pl.when(cond)(go)

    turns = ((step_x, step_y), (step_y, step_x))
    for half in range(2):
        first, second = turns[half]
        put(z + 1 < depth, half, me, me + 8, 0, own=True)
        put(z > 0, half, me, me - 8, 1, own=True)
        put(None, half, me, me + first, 2, own=True)
        put(None, half, me, me + second, 3, own=True)
        put(None, half, me, me + step_core, 4, own=True)

    def w_copy(j, kind):
        dest = lax.rem(me + j, count)
        src, dst = w_ends(kind, dest)
        return pltpu.make_async_remote_copy(
            src_ref=src,
            dst_ref=dst,
            send_sem=w_send.at[kind, j],
            recv_sem=w_recv.at[kind, j],
            device_id={"tok": dest},
            device_id_type=pl.DeviceIdType.MESH,
        )

    def send_weights(distance):
        kinds = [kind for kind in range(3) if min(1 + kind // 2, depth - 1) == distance]
        if kinds:

            @pl.loop(1, count)
            def _(j):
                for kind in kinds:
                    w_copy(j, kind).start()

    send_weights(0)

    def both_ways(distance):
        yield (z >= distance, -8 * distance)
        if distance:
            yield (z + distance < depth, 8 * distance)

    def from_first(distance):
        for half in range(2):
            first, second = turns[half]
            for cond, shift in both_ways(distance):
                block = me + first + shift
                arrived(cond, half, block)
                put(cond, half, block, me + second, 3)
                put(cond, half, block, me + step_core, 4)

    for distance in range(1, depth):
        for half in range(2):
            first, second = turns[half]
            for cond, shift in both_ways(distance):
                block = me + shift
                arrived(cond, half, block)
                if shift < 0:
                    put(jnp.logical_and(cond, z + 1 < depth), half, block, me + 8, 0)
                else:
                    put(jnp.logical_and(cond, z > 0), half, block, me - 8, 1)
                put(cond, half, block, me + first, 2)
                put(cond, half, block, me + second, 3)
                put(cond, half, block, me + step_core, 4)
        send_weights(distance)
        from_first(distance - 1)
    from_first(depth - 1)
    own_tok.wait()
    for copy in own_w:
        copy.wait()

    @pl.loop(1, count)
    def _(j):
        for kind in range(3):
            w_copy(j, kind).wait_recv()

    def last_leg(turn):
        distance = (turn + 1) // 2
        there = z + distance * (1 - 2 * lax.rem(turn, 2))
        return there, jnp.logical_and(there >= 0, there < depth)

    def to_core(half, there, base):
        block = there * 8 + lax.rem(me, 8) + base
        return tok_copy(half, block, me + step_core, 4)

    def load(there, k):
        block = there * 8 + 2 * lax.rem(k, 4) + jnp.where(k < 4, core, 1 - core)
        return block, pltpu.make_async_copy(all_tok.at[block], held.at[k], held_sem.at[k])

    block_rows = tok_ref.shape[0]

    @pl.loop(0, 2 * depth - 1)
    def _(turn):
        there, valid = last_leg(turn)

        @pl.when(valid)
        def _():
            for half in range(2):
                first, second = turns[half]
                for base in (second, first + second):
                    to_core(half, there, base).wait_recv()
                    to_core(half, there, base).start()

            @pl.loop(0, 4)
            def _(k):
                load(there, k)[1].start()

            @pl.loop(0, 8)
            def _(k):
                block, copy = load(there, k)

                @pl.when(k == 1)
                def _():
                    @pl.loop(0, 4)
                    def _(other):
                        later, later_copy = load(there, other + 4)
                        for half in range(2):
                            tok_copy(half, later, me, 0).wait_recv()
                        later_copy.start()

                copy.wait()
                place = pl.ds(pl.multiple_of(block * block_rows, block_rows), block_rows)
                raw_ref[place, :] = jnp.dot(
                    held[k], columns[...], preferred_element_type=jnp.float32
                )

    @pl.loop(0, 2 * depth - 1)
    def _(turn):
        there, valid = last_leg(turn)

        @pl.when(valid)
        def _():
            for half in range(2):
                first, second = turns[half]
                for base in (second, first + second):
                    to_core(half, there, base).wait_send()

    for cond, half, block, dest, slot in sent:

        def done(half=half, block=block, dest=dest, slot=slot):
            tok_copy(half, block, dest, slot).wait_send()

        done() if cond is None else pl.when(cond)(done)

    @pl.loop(1, count)
    def _(j):
        for kind in range(3):
            w_copy(j, kind).wait_send()


def exchanged(tokens, weights):
    count = lax.axis_size("tok")
    rows, width = tokens.shape
    w_rows, channels = weights[0].shape
    cols = 3 * channels // count
    anywhere = pl.BlockSpec(memory_space=pl.ANY)
    raw, _ = pl.pallas_call(
        functools.partial(exchange_kernel, count),
        out_shape=(
            jax.ShapeDtypeStruct((count * rows, cols), jnp.float32),
            jax.ShapeDtypeStruct((count, rows, width), tokens.dtype),
        ),
        in_specs=[anywhere] * 4,
        out_specs=(pl.BlockSpec(memory_space=pltpu.VMEM), anywhere),
        scratch_shapes=[
            pltpu.VMEM((count * w_rows, cols), weights[0].dtype),
            pltpu.VMEM((8, rows, width), tokens.dtype),
            pltpu.SemaphoreType.DMA((2, count // 2, 5)),
            pltpu.SemaphoreType.DMA((2, count)),
            pltpu.SemaphoreType.DMA((3, count)),
            pltpu.SemaphoreType.DMA((3, count)),
            pltpu.SemaphoreType.DMA((4,)),
            pltpu.SemaphoreType.DMA((8,)),
        ],
        compiler_params=pltpu.CompilerParams(
            collective_id=0, has_side_effects=True, vmem_limit_bytes=40 * 2**20
        ),
    )(tokens, *weights)
    return raw


def projected(tokens, weights):
    count = lax.axis_size("tok")
    rows = tokens.shape[0]
    w_rows, channels = weights[0].shape
    if count % 8 == 0 and rows % 32 == 0 and w_rows % 16 == 0 and channels % (128 * count) == 0:
        return exchanged(tokens, weights)
    gathered = lax.all_gather(tokens, "tok", axis=0, tiled=True)
    columns = [
        lax.all_to_all(weight, "tok", split_axis=1, concat_axis=0, tiled=True)
        for weight in weights
    ]
    return jnp.dot(
        gathered, jnp.concatenate(columns, axis=1), preferred_element_type=jnp.float32
    )


def short_rows(raw, taps):
    padded = jnp.pad(raw, ((2, 0), (0, 0)))
    return taps[0] * raw + taps[1] * padded[1:-1] + taps[2] * padded[:-2]


def local_by_channels(tokens, w_query, w_key, w_value, short_taps, filters, skip_gain):
    owned = filters.shape[0]
    start = lax.axis_index("tok") * owned
    raw = projected(tokens, (w_query, w_key, w_value))
    raw = [raw[:, kind * owned : (kind + 1) * owned] for kind in range(3)]
    taps = lax.dynamic_slice_in_dim(short_taps, start, owned, axis=2)
    query = short_rows(raw[0], taps[0]).astype(jnp.bfloat16)
    key_value = (short_rows(raw[1], taps[1]) * short_rows(raw[2], taps[2])).astype(jnp.bfloat16)
    outer, inner = balanced(filters.shape[1])
    tables = quarter_tables(outer, inner)
    convolved = long_conv(key_value, filters.T, tables, outer, inner)
    mixed = (convolved + skip_gain[None, :] * key_value.astype(jnp.float32)).astype(jnp.bfloat16)
    result = (query.astype(jnp.float32) * mixed.astype(jnp.float32)).astype(jnp.bfloat16)
    return lax.all_to_all(result, "tok", split_axis=0, concat_axis=1, tiled=True)


def solution(mesh):
    in_specs = (
        P("tok", "tp"),
        P("tok", "tp"),
        P("tok", "tp"),
        P("tok", "tp"),
        P(None, None, "tp"),
        P(("tp", "tok"), None),
        P(("tp", "tok")),
    )
    out_specs = P("tok", "tp")
    local = local_by_channels if mesh.shape["tp"] == 1 else local_by_tokens
    return jax.shard_map(local, mesh=mesh, in_specs=in_specs, out_specs=out_specs, check_vma=False)
```
